32 devices in a mesh: line: 4 (over y, core), bus: 8 (over z, x).
Axes of the slice: x: 2, y: 2, z: 4, core: 2. Of those that a mesh axis runs over, the one named last changes fastest.
Arguments:
- site_values: float32 [512, 32768], P('line', 'bus'), may hold values from -6 to 6
- site_bus: int32 [32768], replicated, may hold values from 0 to 71679, as said below
- block_count: int32 [88, 8], P('line', 'bus'), may hold values from 0 to 3
- block_zone: int32 [88, 24], P('line', 'bus'), may hold values from 0 to 13, as said below
- ptdf_blocks: bfloat16 [88, 24, 512, 640], P('line', 'bus'), may hold values from -0.078125 to 0.078125
- rating: float32 [45056], P('line'), may hold values from 0.5 to 4
Outputs:
- loading: float32 [512, 45056], P('bus', 'line')
- worst: float32 [45056], P('line')
The draws below stay inside these ranges and needn't reach their ends.
Inputs may be any that keep to these rules, and one draw needn't show every extreme that they name: `site_bus`: every aligned block of 4096 sites holds exactly 512 sites whose bus lies in each bus group, the range of 8960 consecutive buses; bus 0 and the last bus each carry a site. `block_zone`: for each line zone, the 3 slots of one bus group name distinct zones of that group.
All inputs are finite; a program needn't handle non-finite values.
Results may differ from the reference program's by a relative error of at most 0.015.
Values may be sent and summed in bfloat16 or wider, within the bound.
No kernel may reach another device: no remote copies, remote signals or barrier semaphores. Data moves between devices by JAX's collectives and lax.ppermute only.
A program may use at most 128 MiB of HBM per device.

```python
import math
import jax
import jax.numpy as jnp
from jax import lax

NB = 71680
NL = 45056
ZL = 512
ZB = 640
CAP = 3
SCEN = 512
SITE_DEV = 4096
LZ = 88
BZ = 112
BZD = 14
BUS_DEV = 8960
SITES = 32768
N_BUS = 8


def draw_site_bus(key, part):
    group_total = SITES // SITE_DEV
    first, second = jax.random.split(jax.random.fold_in(key, 11), 2)
    base = jnp.repeat(jnp.arange(group_total, dtype=jnp.int32), SITE_DEV // group_total)
    block_keys = jax.random.split(first, group_total)
    shuffled = jax.vmap(lambda k: jax.random.permutation(k, base))(block_keys)
    offset = jax.random.randint(second, (group_total, SITE_DEV), 0, BUS_DEV, dtype=jnp.int32)
    flat = (shuffled * BUS_DEV + offset).reshape(SITES).astype(jnp.int32)
    groups = flat // BUS_DEV
    high_pos = jnp.argmax(groups == group_total - 1)
    low_pos = jnp.argmax(groups == 0)
    flat = flat.at[high_pos].set(NB - 1)
    flat = flat.at[low_pos].set(0)
    return flat.astype(jnp.int32)


def draw_block_zone(key, part):
    group_total = NB // BUS_DEV
    keys = jax.random.split(jax.random.fold_in(key, 23), LZ * group_total)
    picks = jax.vmap(lambda k: jax.random.permutation(k, BZD)[:CAP])(keys)
    return picks.reshape(LZ, group_total * CAP).astype(jnp.int32)


def touch_ends(result, own_key, smallest, top_value):
    index_at = [jax.random.randint(jax.random.fold_in(own_key, axis), (), 0, length) for axis, length in enumerate(result.shape)]
    widest = result.shape.index(max(result.shape))
    next_to = index_at[:widest] + [(index_at[widest] + 1) % result.shape[widest]] + index_at[widest + 1:]
    return result.at[tuple(index_at)].set(smallest).at[tuple(next_to)].set(top_value)


def block_levels(own_key, extent, pieces, smallest, top_value):
    def one(axis_at, blocks):
        heights = jax.random.uniform(jax.random.fold_in(jax.random.fold_in(own_key, 6), axis_at), (blocks,), jnp.float32, smallest / len(pieces), top_value / len(pieces))
        return jnp.repeat(jnp.exp(heights), extent[axis_at] // blocks).reshape((-1,) + (1,) * (len(extent) - axis_at - 1))

    gain = one(*pieces[0])
    for cut in pieces[1:]:
        gain = gain * one(*cut)
    return gain


def noise(rng, shape, deviation, bound, cuts=(), kind=jnp.bfloat16):
    drawn = jax.random.normal(rng, shape, jnp.float32) * deviation
    if len(cuts) > 0:
        drawn = block_levels(rng, shape, cuts, -0.22, 0.18) * drawn
    return jnp.clip(drawn, min=-bound, max=bound).astype(kind)


def setup_inputs(seed: int = 0) -> dict:
    key_list = jax.random.split(jax.random.key(seed), 7)
    return {
        "site_values": noise(key_list[0], (SCEN, SITES), 1.0, 6.0, ((0, 4), (1, 8)), jnp.float32),
        "site_bus": draw_site_bus(jax.random.fold_in(key_list[6], 71), 0),
        "block_count": touch_ends(jax.random.randint(key_list[2], (LZ, N_BUS), 0, CAP + 1), jax.random.fold_in(key_list[2], 1), 0, CAP).astype(jnp.int32),
        "block_zone": draw_block_zone(jax.random.fold_in(key_list[6], 71), 0),
        "ptdf_blocks": noise(key_list[4], (LZ, N_BUS * CAP, ZL, ZB), (ZB * N_BUS) ** -0.5, 0.078125, ((0, 4), (1, 8))),
        "rating": jnp.clip(jnp.exp(math.log(4.0) - 2.0794415 * jax.random.uniform(key_list[5], (NL,), jnp.float32) ** block_levels(key_list[5], (NL,), ((0, 4),), -0.2, 0.2)), 0.5, 4.0),
    }


def reference(site_values, site_bus, block_count, block_zone, ptdf_blocks, rating):
    summed = jnp.zeros((SCEN, NB), jnp.float32).at[:, site_bus].add(site_values.astype(jnp.float32))
    injection = summed.astype(jnp.bfloat16)
    inj_zones = injection.astype(jnp.float32).reshape(SCEN, BZ, ZB)
    slot_ids = jnp.arange(N_BUS * CAP).astype(jnp.int32)
    offsets = ((slot_ids // CAP) * BZD).astype(jnp.int32)

    def one_zone(carry, inputs):
        counts, zones, blocks = inputs
        global_zone = (offsets + zones).astype(jnp.int32)
        live = ((slot_ids % CAP) < jnp.repeat(counts, CAP)).astype(jnp.float32).reshape(N_BUS, CAP)
        picked = jnp.take(inj_zones, global_zone, axis=1).reshape(SCEN, N_BUS, CAP, ZB)
        grouped = blocks.astype(jnp.float32).reshape(N_BUS, CAP, ZL, ZB)
        parts = jnp.einsum("sgcb,gclb,gc->sgl", picked, grouped, live)
        rounded = lax.optimization_barrier(parts.astype(jnp.bfloat16))
        flow = jnp.sum(rounded.astype(jnp.float32), axis=1)
        return carry, flow

    _, flows = lax.scan(one_zone, jnp.float32(0.0), (block_count, block_zone, ptdf_blocks))
    flow = jnp.transpose(flows, (1, 0, 2)).reshape(SCEN, NL)
    loading = flow / rating[None, :]
    worst = jnp.max(jnp.abs(loading), axis=0)
    return loading, worst
```

```python
import functools

import jax
import jax.numpy as jnp
from jax import lax
from jax.experimental import pallas as pl
from jax.experimental.pallas import tpu as pltpu
from jax.sharding import PartitionSpec as P

NB = 71680
TILE = 256
VMEM = 48 * 1024 * 1024
F32 = jnp.float32
BF16 = jnp.bfloat16


def params(n):
    return pltpu.CompilerParams(dimension_semantics=("arbitrary",) * n, vmem_limit_bytes=VMEM)


def cost(flops, nbytes):
    return pl.CostEstimate(flops=int(flops), bytes_accessed=int(nbytes), transcendentals=0)


def hot(ids, first, rows):
    at = lax.broadcasted_iota(jnp.int32, (rows, ids.shape[1]), 0) + first
    return (at == ids).astype(F32).astype(BF16)


def route_kernel(order_ref, values_ref, out_ref, rounded):
    @pl.when(pl.program_id(0) == 0)
    def _():
        rounded[...] = values_ref[...].astype(BF16)

    depth = values_ref.shape[1]
    step = 512
    ids = order_ref[0]
    total = jnp.zeros(out_ref.shape[1:], F32)
    for at in range(0, depth, step):
        total += jnp.dot(
            rounded[:, at : at + step], hot(ids, at, step), preferred_element_type=F32
        )
    out_ref[0] = total.astype(BF16)


def route(order, values):
    groups, _, width = order.shape
    rows, depth = values.shape
    return pl.pallas_call(
        route_kernel,
        grid=(groups,),
        in_specs=[
            pl.BlockSpec((1, 1, width), lambda g: (g, 0, 0)),
            pl.BlockSpec((rows, depth), lambda g: (0, 0)),
        ],
        out_specs=pl.BlockSpec((1, rows, width), lambda g: (g, 0, 0)),
        out_shape=jax.ShapeDtypeStruct((groups, rows, width), BF16),
        scratch_shapes=[pltpu.VMEM((rows, depth), BF16)],
        compiler_params=params(1),
        cost_estimate=cost(4 * rows * depth * groups * width, 4 * rows * depth),
        name="route",
    )(order, values)


def merge_kernel(order_ref, runs_ref, out_ref):
    runs, rows, width = runs_ref.shape
    ids = order_ref[0]
    total = jnp.zeros((rows, ids.shape[1]), F32)
    for run in range(runs):
        total += jnp.dot(runs_ref[run], hot(ids, run * width, width), preferred_element_type=F32)
    total = total.astype(BF16)
    for part in range(out_ref.shape[0]):
        out_ref[part] = total[:, part * TILE : (part + 1) * TILE]


def merge(order, runs):
    count, rows, width = runs.shape
    sites = count * width
    step = 2 * TILE
    return pl.pallas_call(
        merge_kernel,
        grid=(sites // step,),
        in_specs=[
            pl.BlockSpec((1, 1, step), lambda t: (t, 0, 0)),
            pl.BlockSpec((count, rows, width), lambda t: (0, 0, 0)),
        ],
        out_specs=pl.BlockSpec((step // TILE, rows, TILE), lambda t: (t, 0, 0)),
        out_shape=jax.ShapeDtypeStruct((sites // TILE, rows, TILE), BF16),
        compiler_params=params(1),
        cost_estimate=cost(4 * rows * sites * sites, 4 * rows * sites),
        name="merge",
    )(order.reshape(sites // step, 1, step), runs)


def inject_kernel(first_ref, last_ref, rows_ref, ids_ref, *refs):
    pieces, out_ref, total = refs[:-2], refs[-2], refs[-1]
    zone = pl.program_id(0)
    scen, width = total.shape
    total[...] = jnp.zeros_like(total)

    @pl.loop(first_ref[zone], last_ref[zone])
    def _(t):
        at = lax.broadcasted_iota(jnp.int32, (width, TILE), 0) + zone * width
        table = (at == ids_ref[t]).astype(F32).astype(BF16)
        part = jnp.concatenate([piece[t] for piece in pieces], axis=0)
        total[...] += lax.dot_general(
            part, table, (((1,), (1,)), ((), ())), preferred_element_type=F32
        )

    blocks = rows_ref.shape[0]
    high = scen // blocks
    for j in range(blocks):
        rows = pl.ds(pl.multiple_of(rows_ref[j] * high, high), high)
        out_ref[0, j * high : (j + 1) * high] = total[rows, :].astype(BF16)


def inject(first, last, row_blocks, ids, pieces, zones, width):
    tiles, rows, _ = pieces[0].shape
    scen = rows * len(pieces)
    whole = pl.BlockSpec((tiles, rows, TILE), lambda z, *_: (0, 0, 0))
    return pl.pallas_call(
        inject_kernel,
        grid_spec=pltpu.PrefetchScalarGridSpec(
            num_scalar_prefetch=3,
            grid=(zones,),
            in_specs=[pl.BlockSpec((tiles, 1, TILE), lambda z, *_: (0, 0, 0))]
            + [whole] * len(pieces),
            out_specs=pl.BlockSpec((1, scen, width), lambda z, *_: (z, 0, 0)),
            scratch_shapes=[pltpu.VMEM((scen, width), F32)],
        ),
        out_shape=jax.ShapeDtypeStruct((zones, scen, width), BF16),
        compiler_params=params(1),
        cost_estimate=cost(4 * scen * width * TILE * (tiles + zones), 2 * zones * scen * width),
        name="inject",
    )(first, last, row_blocks, ids, *pieces)


def flow_kernel(count_ref, zone_ref, inj_ref, block_ref, *refs, base):
    outs, total = refs[:-1], refs[-1]
    z, k = pl.program_id(0), pl.program_id(1)
    live = k < count_ref[z + base]

    @pl.when(k == 0)
    def _():
        total[...] = jnp.zeros_like(total)

    @pl.when(live)
    def _():
        total[...] += lax.dot_general(
            inj_ref[0], block_ref[0, 0], (((1,), (1,)), ((), ())), preferred_element_type=F32
        )

    @pl.when(k == pl.num_programs(1) - 1)
    def _():
        row = 0
        for out in outs:
            out[...] = total[row : row + out.shape[0], :].astype(BF16)
            row += out.shape[0]


def partial_flow(count, zone, inj, blocks, base, zones, splits):
    _, slots, lines, width = blocks.shape
    scen = inj.shape[1]

    def slot(z, k, count):
        return jnp.minimum(k, jnp.maximum(count[z + base] - 1, 0))

    return pl.pallas_call(
        functools.partial(flow_kernel, base=base),
        grid_spec=pltpu.PrefetchScalarGridSpec(
            num_scalar_prefetch=2,
            grid=(zones, slots),
            in_specs=[
                pl.BlockSpec(
                    (1, scen, width),
                    lambda z, k, count, zone: (
                        zone[(z + base) * slots + slot(z, k, count)],
                        0,
                        0,
                    ),
                ),
                pl.BlockSpec(
                    (1, 1, lines, width),
                    lambda z, k, count, zone: (z + base, slot(z, k, count), 0, 0),
                ),
            ],
            out_specs=[pl.BlockSpec((rows, lines), lambda z, k, *_: (0, z)) for rows in splits],
            scratch_shapes=[pltpu.VMEM((scen, lines), F32)],
        ),
        out_shape=[jax.ShapeDtypeStruct((rows, zones * lines), BF16) for rows in splits],
        compiler_params=params(2),
        cost_estimate=cost(
            zones * slots * scen * lines * width, zones * slots * (scen + lines) * width
        ),
        name="partial_flow",
    )(count, zone.reshape(-1), inj, blocks)


def chunks_of(zones):
    sizes = []
    for size in (1, 2):
        if zones - sum(sizes) > size:
            sizes.insert(0, size)
    left = zones - sum(sizes)
    while left > 0:
        sizes.insert(0, min(4, left))
        left -= sizes[0]
    return sizes


def add(*terms):
    return sum(term.astype(F32) for term in terms)


def body(site_values, site_bus, block_count, block_zone, ptdf_blocks, rating):
    here = lax.axis_index("bus")
    groups = lax.axis_size("bus")
    lines_size = lax.axis_size("line")
    scen_part, site_dev = site_values.shape
    bus_dev = NB // groups
    per_group = site_dev // groups
    group_sites = groups * per_group
    zones_dev, slots_dev, line_zone, zone_width = ptdf_blocks.shape
    bus_zones = bus_dev // zone_width
    scen = scen_part * lines_size
    high = scen // groups

    own_ids = lax.dynamic_slice_in_dim(site_bus, here * site_dev, site_dev)
    keys = lax.sort(own_ids * site_dev + jnp.arange(site_dev, dtype=jnp.int32))
    order = (keys % site_dev).reshape(groups, 1, per_group)
    sorted_bus = (keys // site_dev).reshape(groups, per_group)
    got_bus = lax.all_to_all(sorted_bus, "bus", 0, 0, tiled=True)
    got = lax.all_to_all(route(order, site_values), "bus", 0, 0, tiled=True)

    local = (got_bus - here * bus_dev).reshape(group_sites)
    keys = lax.sort(local * group_sites + jnp.arange(group_sites, dtype=jnp.int32))
    local = keys // group_sites
    sites = merge(keys % group_sites, got)
    edges = jnp.arange(bus_zones + 1, dtype=jnp.int32) * zone_width
    starts = jnp.sum((local[None, :] < edges[:, None]).astype(jnp.int32), axis=1)
    first = starts[:-1] // TILE
    last = (starts[1:] + TILE - 1) // TILE
    ids = local.reshape(group_sites // TILE, 1, TILE)

    tuned = groups == 8 and lines_size == 4 and scen_part == 2 * high
    if tuned:
        me = lax.axis_index("line")
        by_core = [(i, i ^ 1) for i in range(lines_size)]
        by_y = [(i, i ^ 2) for i in range(lines_size)]
        across = lax.ppermute(sites, "line", by_y)
        pieces = [
            sites,
            lax.ppermute(sites, "line", by_core),
            across,
            lax.ppermute(across, "line", by_core),
        ]
        x, z = here % 2, here // 2
        slots = jnp.arange(4, dtype=jnp.int32)
        z_dest = jnp.where(z < 2, slots, 3 - slots)
        piece_at = (z_dest ^ me) * 2
        row_blocks = jnp.concatenate([piece_at + (1 - x), piece_at + x])
        splits = (scen // 2, scen // 2)
    else:
        gathered = lax.all_gather(sites, "line", axis=0)
        pieces = [gathered[i] for i in range(lines_size)]
        row_blocks = jnp.arange(groups, dtype=jnp.int32)
        splits = (scen,)

    inj = inject(first, last, row_blocks.astype(jnp.int32), ids, pieces, bus_zones, zone_width)
    count = block_count[:, 0]

    if tuned:
        swap_x = [(i, i ^ 1) for i in range(8)]
        inward = [(0, 2), (1, 3), (6, 4), (7, 5)]
        middle = [(2, 4), (3, 5), (4, 2), (5, 3)]
        outward = [(2, 0), (3, 1), (4, 6), (5, 7)]
        inner = (z == 1) | (z == 2)
        flows = []
        base = 0
        for zones in chunks_of(zones_dev):
            send, keep = partial_flow(
                count, block_zone, inj, ptdf_blocks, base, zones, splits
            )
            base += zones
            summed = add(keep, lax.ppermute(send, "bus", swap_x)).astype(BF16)
            own0, own1, own23 = summed[:high], summed[high : 2 * high], summed[2 * high :]
            from1 = lax.ppermute(own1, "bus", inward)
            from23 = lax.ppermute(own23, "bus", inward)
            mid = lax.ppermute(add(own23, from23).astype(BF16), "bus", middle)
            end = lax.ppermute(add(own0, mid[high:]).astype(BF16), "bus", outward)
            flows.append(
                jnp.where(inner, add(own1, from1, mid[:high]), add(own0, end))
            )
        flow = jnp.concatenate(flows, axis=1)
    else:
        (whole,) = partial_flow(
            count, block_zone, inj, ptdf_blocks, 0, zones_dev, splits
        )
        flow = lax.psum_scatter(whole, "bus", scatter_dimension=0, tiled=True).astype(F32)

    loading = flow / rating[None, :]
    worst = jnp.max(jnp.abs(loading), axis=0)
    if groups & (groups - 1) == 0:
        step = 1
        while step < groups:
            pairs = [(i, i ^ step) for i in range(groups)]
            worst = jnp.maximum(worst, lax.ppermute(worst, "bus", pairs))
            step *= 2
    else:
        worst = lax.pmax(worst, "bus")
    return loading, worst


def solution(mesh):
    return jax.shard_map(
        body,
        mesh=mesh,
        in_specs=(
            P("line", "bus"),
            P(),
            P("line", "bus"),
            P("line", "bus"),
            P("line", "bus", None, None),
            P("line"),
        ),
        out_specs=(P("bus", "line"), P("line")),
        check_vma=False,
    )
```

```python
import functools

import jax
import jax.numpy as jnp
from jax import lax
from jax.experimental import pallas as pl
from jax.experimental.pallas import tpu as pltpu
from jax.sharding import PartitionSpec as P

NB = 71680
TILE = 128
WINDOW = 4
EARLY = 8
STEP = 2
F32 = jnp.float32
BF16 = jnp.bfloat16


def params(n, mib=16):
    return pltpu.CompilerParams(
        dimension_semantics=("arbitrary",) * n, vmem_limit_bytes=mib * 1024 * 1024
    )


def cost(flops, nbytes):
    return pl.CostEstimate(flops=int(flops), bytes_accessed=int(nbytes), transcendentals=0)


def hot(ids, first, rows):
    at = lax.broadcasted_iota(jnp.int32, (rows, ids.shape[1]), 0) + first
    return (at == ids).astype(F32).astype(BF16)


def down(row):
    return jnp.broadcast_to(row, (row.shape[1], row.shape[1])).T


def hot_rows(ids, first, columns):
    at = lax.broadcasted_iota(jnp.int32, ids.shape, 1) + first
    tables = [
        (ids == at + c).astype(F32).astype(BF16) for c in range(0, columns, ids.shape[1])
    ]
    return jnp.concatenate(tables, axis=1)


def running_count(mask, part):
    rows, lanes = mask.shape
    mask = mask.astype(F32).astype(BF16)
    up_to = lax.broadcasted_iota(jnp.int32, (lanes, lanes), 0) <= lax.broadcasted_iota(
        jnp.int32, (lanes, lanes), 1
    )
    inside = jnp.dot(mask, up_to.astype(F32).astype(BF16), preferred_element_type=F32)
    r = lax.broadcasted_iota(jnp.int32, (rows, rows), 0)
    c = lax.broadcasted_iota(jnp.int32, (rows, rows), 1)
    earlier = ((c < r) & ((c ^ r) < part)).astype(F32).astype(BF16)
    before = jnp.dot(earlier, mask, preferred_element_type=F32)
    return (inside + jnp.sum(before, axis=1, keepdims=True)).astype(jnp.int32)


def route_kernel(here_ref, bus_ref, values_ref, out_ref, rounded, places, *, groups, bus_dev):
    del here_ref
    group = pl.program_id(0)
    width = out_ref.shape[2]
    rows = bus_ref.shape[0]

    @pl.when(group == 0)
    def _():
        rounded[...] = values_ref[...].astype(BF16)
        ids = bus_ref[...]
        masks = [(ids >= g * bus_dev) & (ids < (g + 1) * bus_dev) for g in range(groups)]
        masks = jnp.concatenate([mask.astype(F32) for mask in masks], axis=0)
        count = running_count(masks, rows)
        place = jnp.zeros(ids.shape, jnp.int32)
        for g in range(groups):
            part = slice(g * rows, (g + 1) * rows)
            place += jnp.where(masks[part] > 0, count[part] + (g * width - 1), 0)
        for r in range(rows):
            places[r * TILE : (r + 1) * TILE] = down(place[r : r + 1])

    total = jnp.zeros(out_ref.shape[1:], F32)
    step = 4 * TILE
    for at in range(0, rows * TILE, step):
        table = hot_rows(places[at : at + step], group * width, width)
        total += jnp.dot(rounded[:, at : at + step], table, preferred_element_type=F32)
    out_ref[0] = total.astype(BF16)


def route(here, site_bus, values, groups, bus_dev):
    scen, depth = values.shape
    width = depth // groups
    rows = depth // TILE
    return pl.pallas_call(
        functools.partial(route_kernel, groups=groups, bus_dev=bus_dev),
        grid_spec=pltpu.PrefetchScalarGridSpec(
            num_scalar_prefetch=1,
            grid=(groups,),
            in_specs=[
                pl.BlockSpec((rows, TILE), lambda g, here: (here[0], 0)),
                pl.BlockSpec((scen, depth), lambda g, here: (0, 0)),
            ],
            out_specs=pl.BlockSpec((1, scen, width), lambda g, here: (g, 0, 0)),
            scratch_shapes=[pltpu.VMEM((scen, depth), BF16), pltpu.VMEM((depth, TILE), jnp.int32)],
        ),
        out_shape=jax.ShapeDtypeStruct((groups, scen, width), BF16),
        compiler_params=params(1),
        cost_estimate=cost(4 * scen * depth * depth, 4 * scen * depth),
        name="route",
    )(here.reshape(1), site_bus.reshape(-1, TILE), values)


def arrivals_kernel(here_ref, bus_ref, out_ref, places, local, *, bus_dev):
    block = pl.program_id(0)
    width = out_ref.shape[2]
    rows = bus_ref.shape[0] // pl.num_programs(0)

    @pl.when(block == 0)
    def _():
        ids = bus_ref[...] - here_ref[0] * bus_dev
        mask = (ids >= 0) & (ids < bus_dev)
        places[...] = jnp.where(mask, running_count(mask, rows) - 1, -1)
        local[...] = jnp.where(mask, ids, 0)

    sub = lax.broadcasted_iota(jnp.int32, (16, TILE), 0)
    total = jnp.zeros((16, width), F32)
    step = 4
    for at in range(0, rows, step):
        tables, parts = [], []
        for r in range(at, at + step):
            row = pl.ds(block * rows + r, 1)
            tables.append(hot_rows(down(places[row]), 0, width))
            ids = local[row]
            part = jnp.where(sub == 0, ids >> 7, jnp.where(sub == 1, ids & 127, 0))
            parts.append(part.astype(F32).astype(BF16))
        total += jnp.dot(
            jnp.concatenate(parts, axis=1),
            jnp.concatenate(tables, axis=0),
            preferred_element_type=F32,
        )
    out_ref[0] = (total[0:1] * 128.0 + total[1:2]).astype(jnp.int32)


def arrivals(here, site_bus, groups, site_dev, bus_dev):
    width = site_dev // groups
    rows = site_bus.shape[0] // TILE
    return pl.pallas_call(
        functools.partial(arrivals_kernel, bus_dev=bus_dev),
        grid_spec=pltpu.PrefetchScalarGridSpec(
            num_scalar_prefetch=1,
            grid=(groups,),
            in_specs=[pl.BlockSpec((rows, TILE), lambda g, here: (0, 0))],
            out_specs=pl.BlockSpec((1, 1, width), lambda g, here: (g, 0, 0)),
            scratch_shapes=[pltpu.VMEM((rows, TILE), jnp.int32)] * 2,
        ),
        out_shape=jax.ShapeDtypeStruct((groups, 1, width), jnp.int32),
        compiler_params=params(1),
        cost_estimate=cost(4 * 16 * site_dev * site_dev, 4 * rows * TILE),
        name="arrivals",
    )(here.reshape(1), site_bus.reshape(-1, TILE))


def merge_kernel(order_ref, runs_ref, out_ref):
    runs, rows, width = runs_ref.shape
    ids = order_ref[0]
    total = jnp.zeros((rows, ids.shape[1]), F32)
    for run in range(runs):
        total += jnp.dot(runs_ref[run], hot(ids, run * width, width), preferred_element_type=F32)
    total = total.astype(BF16)
    for part in range(out_ref.shape[0]):
        out_ref[part] = total[:, part * TILE : (part + 1) * TILE]


def merge(order, runs):
    count, rows, width = runs.shape
    sites = count * width
    step = 4 * TILE
    return pl.pallas_call(
        merge_kernel,
        grid=(sites // step,),
        in_specs=[
            pl.BlockSpec((1, 1, step), lambda t: (t, 0, 0)),
            pl.BlockSpec((count, rows, width), lambda t: (0, 0, 0)),
        ],
        out_specs=pl.BlockSpec((step // TILE, rows, TILE), lambda t: (t, 0, 0)),
        out_shape=jax.ShapeDtypeStruct((sites // TILE, rows, TILE), BF16),
        compiler_params=params(1),
        cost_estimate=cost(4 * rows * sites * sites, 4 * rows * sites),
        name="merge",
    )(order.reshape(sites // step, 1, step), runs)


def inject_kernel(first_ref, windows_ref, rows_ref, ids_ref, *refs):
    pieces, out_ref, total, places = refs[:-3], refs[-3], refs[-2], refs[-1]
    zone = pl.program_id(0)
    scen, width = total.shape
    tiles = ids_ref.shape[0]

    @pl.when(zone == 0)
    def _():
        for t in range(tiles):
            places[t] = down(ids_ref[t])

    def window(w):
        parts, tables = [], []
        for j in range(WINDOW):
            t = first_ref[zone] + w * WINDOW + j
            at = jnp.minimum(t, tiles - 1)
            ids = jnp.where(t < tiles, places[at], -1)
            tables.append(hot_rows(ids, zone * width, width))
            parts.append(jnp.concatenate([piece[at] for piece in pieces], axis=0))
        return jnp.dot(
            jnp.concatenate(parts, axis=1),
            jnp.concatenate(tables, axis=0),
            preferred_element_type=F32,
        )

    total[...] = window(0)

    @pl.loop(1, windows_ref[zone])
    def _(w):
        total[...] += window(w)

    blocks = rows_ref.shape[0]
    high = scen // blocks
    for j in range(blocks):
        rows = pl.ds(pl.multiple_of(rows_ref[j] * high, high), high)
        out_ref[0, j * high : (j + 1) * high] = total[rows, :].astype(BF16)


def inject(first, windows, row_blocks, ids, pieces, zones, width):
    tiles, rows, _ = pieces[0].shape
    scen = rows * len(pieces)
    whole = pl.BlockSpec((tiles, rows, TILE), lambda z, *_: (0, 0, 0))
    return pl.pallas_call(
        inject_kernel,
        grid_spec=pltpu.PrefetchScalarGridSpec(
            num_scalar_prefetch=3,
            grid=(zones,),
            in_specs=[pl.BlockSpec((tiles, 1, TILE), lambda z, *_: (0, 0, 0))]
            + [whole] * len(pieces),
            out_specs=pl.BlockSpec((1, scen, width), lambda z, *_: (z, 0, 0)),
            scratch_shapes=[
                pltpu.VMEM((scen, width), F32),
                pltpu.VMEM((tiles, TILE, TILE), jnp.int32),
            ],
        ),
        out_shape=jax.ShapeDtypeStruct((zones, scen, width), BF16),
        compiler_params=params(1),
        cost_estimate=cost(1 << 16, 1 << 10),
        name="inject",
    )(first, windows, row_blocks, ids, *pieces)


def sum_x(give, own, received):
    rows = give.shape[0]
    return (
        add(give[...], received[:rows]).astype(BF16),
        add(own[...], received[rows:]).astype(BF16),
    )


def sum_z(own, received, near, high):
    mine = add(own[...], received[...]).astype(BF16)
    if mine.shape[0] == high:
        return mine, mine
    low, top = mine[:high], mine[high:]
    return jnp.where(near, top, low), jnp.where(near, low, top)


def run_stages(taken, outs, near, high):
    if taken[0]:
        for result in sum_x(*taken[0]):
            next(outs)[...] = result
    if taken[1]:
        for result in sum_z(*taken[1], near, high):
            next(outs)[...] = result
    if taken[2]:
        next(outs)[...] = add(taken[2][0][...], taken[2][1][...])


def stage_shapes(stages, high):
    shapes = [jax.ShapeDtypeStruct(array.shape, BF16) for array in stages[0][:2]]
    shapes += [jax.ShapeDtypeStruct((high, array.shape[1]), BF16) for array in stages[1]]
    return shapes + [jax.ShapeDtypeStruct(array.shape, F32) for array in stages[2][:1]]


def sums_kernel(near_ref, *refs, stages, high):
    extra = iter(refs)
    taken = [[next(extra) for _ in range(count)] for count in stages]
    run_stages(taken, extra, near_ref[0] == 1, high)


def sums(near, stages, high):
    vmem = pl.BlockSpec(memory_space=pltpu.VMEM)
    shapes = stage_shapes(stages, high)
    return pl.pallas_call(
        functools.partial(sums_kernel, stages=[len(stage) for stage in stages], high=high),
        in_specs=[pl.BlockSpec(memory_space=pltpu.SMEM)] + [vmem] * sum(map(len, stages)),
        out_specs=[vmem] * len(shapes),
        out_shape=shapes,
        compiler_params=pltpu.CompilerParams(vmem_limit_bytes=32 * 1024 * 1024),
        cost_estimate=cost(1 << 16, 1 << 10),
        name="sums",
    )(near, *[array for stage in stages for array in stage])


def flow_kernel(
    count_ref, zone_ref, last_ref, near_ref, token_ref, *refs, base, slots, halves, splits, stages
):
    inj, blocks = refs[: halves * slots], refs[halves * slots : (halves + 1) * slots]
    extra = iter(refs[(halves + 1) * slots :])
    taken = [[next(extra) for _ in range(count)] for count in stages]
    outs = [next(extra) for _ in splits]

    if any(stages):

        @pl.when(pl.program_id(0) == 0)
        def _():
            run_stages(taken, extra, near_ref[0] == 1, splits[-1][0])

    live = count_ref[pl.program_id(0) + base]
    for count in range(slots + 1):

        @pl.when(live == count)
        def _(count=count):
            if count == 0:
                for out in outs:
                    out[...] = jnp.zeros_like(out)
                return
            for half in range(halves):
                total = sum(
                    lax.dot_general(
                        inj[half * slots + k][0],
                        blocks[k][0, 0],
                        (((1,), (1,)), ((), ())),
                        preferred_element_type=F32,
                    )
                    for k in range(count)
                )
                row = 0
                for out, parts in zip(outs, splits):
                    at = half * parts[0]
                    for rows in parts:
                        out[at : at + rows] = total[row : row + rows].astype(BF16)
                        row += rows
                        at += halves * rows


def last_live(count, slots):
    zones = count.shape[0]
    at = jnp.arange(zones, dtype=jnp.int32)[:, None]
    live = jnp.arange(slots, dtype=jnp.int32)[None, :] < count[:, None]
    return lax.cummax(jnp.where(live, at, 0), axis=0).reshape(-1)


def partial_flow(
    count, zone, last, near, token, injs, blocks, base, zones, splits, stages=((), (), ())
):
    _, slots, lines, width = blocks.shape
    scen = injs[0].shape[1]
    halves = len(injs)

    def inj_at(k):
        def at(z, count, zone, last, near):
            return zone[last[(z + base) * slots + k] * slots + k], 0, 0

        return pl.BlockSpec((1, scen, width), at)

    def block_at(k):
        def at(z, count, zone, last, near):
            return last[(z + base) * slots + k], k, 0, 0

        return pl.BlockSpec((1, 1, lines, width), at)

    def whole(array):
        return pl.BlockSpec(array.shape, lambda z, *_: (0, 0))

    high = splits[-1][0]
    shapes = [
        jax.ShapeDtypeStruct((halves * sum(parts), zones * lines), BF16) for parts in splits
    ]
    later = stage_shapes(stages, high)
    extra = [array for stage in stages for array in stage]
    live = zones * slots / 2
    return pl.pallas_call(
        functools.partial(
            flow_kernel,
            base=base,
            slots=slots,
            halves=halves,
            splits=splits,
            stages=[len(stage) for stage in stages],
        ),
        grid_spec=pltpu.PrefetchScalarGridSpec(
            num_scalar_prefetch=4,
            grid=(zones,),
            in_specs=[pl.BlockSpec(memory_space=pl.ANY)]
            + [inj_at(k) for k in range(slots)] * halves
            + [block_at(k) for k in range(slots)]
            + [whole(array) for array in extra],
            out_specs=[
                pl.BlockSpec((halves * sum(parts), lines), lambda z, *_: (0, z))
                for parts in splits
            ]
            + [whole(array) for array in later],
        ),
        out_shape=shapes + later,
        compiler_params=params(1, 32),
        cost_estimate=cost(
            2 * live * halves * scen * lines * width, 2 * live * (halves * scen + lines) * width
        ),
        name="partial_flow",
    )(
        count,
        zone,
        last,
        near,
        token,
        *[inj for inj in injs for _ in range(slots)],
        *[blocks] * slots,
        *extra,
    )


def copy_after(values, token):
    def kernel(values_ref, token_ref, out_ref):
        out_ref[...] = values_ref[...]

    tiles, rows, lanes = values.shape
    block = pl.BlockSpec((tiles // 4, rows, lanes), lambda i: (i, 0, 0))
    return pl.pallas_call(
        kernel,
        grid=(4,),
        in_specs=[block, pl.BlockSpec(memory_space=pl.ANY)],
        out_specs=block,
        out_shape=jax.ShapeDtypeStruct(values.shape, values.dtype),
        compiler_params=params(1),
        cost_estimate=cost(1 << 16, 1 << 10),
        name="copy_after",
    )(values, token)


def cut(first, last, size):
    return [(base, min(size, last - base)) for base in range(first, last, size)]


def add(*terms):
    return sum(term.astype(F32) for term in terms)


def max_over_bus(values, groups):
    if groups & (groups - 1):
        return lax.pmax(values, "bus")
    step = 1
    while step < groups:
        pairs = [(i, i ^ step) for i in range(groups)]
        values = jnp.maximum(values, lax.ppermute(values, "bus", pairs))
        step *= 2
    return values


def body(site_values, site_bus, block_count, block_zone, ptdf_blocks, rating):
    here = lax.axis_index("bus")
    groups = lax.axis_size("bus")
    lines_size = lax.axis_size("line")
    scen_part, site_dev = site_values.shape
    bus_dev = NB // groups
    group_sites = groups * (site_dev // groups)
    zones_dev, slots_dev, line_zone, zone_width = ptdf_blocks.shape
    bus_zones = bus_dev // zone_width
    scen = scen_part * lines_size
    high = scen // groups

    got = lax.all_to_all(
        route(here, site_bus, site_values, groups, bus_dev), "bus", 0, 0, tiled=True
    )

    local = arrivals(here, site_bus, groups, site_dev, bus_dev).reshape(group_sites)
    keys = lax.sort(local * group_sites + jnp.arange(group_sites, dtype=jnp.int32))
    local = keys // group_sites
    edges = jnp.arange(bus_zones + 1, dtype=jnp.int32) * zone_width
    starts = jnp.sum((local[None, :] < edges[:, None]).astype(jnp.int32), axis=1)
    first = starts[:-1] // TILE
    span = WINDOW * TILE
    windows = (starts[1:] - first * TILE + span - 1) // span
    ids = local.reshape(group_sites // TILE, 1, TILE)
    count = block_count[:, 0]
    zone = block_zone.reshape(-1)
    last = last_live(count, slots_dev)
    sites = merge(keys % group_sites, got)

    def injections(row_blocks, pieces):
        return inject(
            first, windows, row_blocks.astype(jnp.int32), ids, pieces, bus_zones, zone_width
        )

    def partial(*call, **options):
        return partial_flow(count, zone, last, *call, **options)

    if groups == 8 and lines_size == 4 and scen_part == 2 * high:
        flows = staged(sites, injections, high, ptdf_blocks, partial)
    else:
        gathered = lax.all_gather(sites, "line", axis=0)
        inj = injections(jnp.arange(groups), [gathered[i] for i in range(lines_size)])
        (whole,) = partial(here.reshape(1), count, [inj], ptdf_blocks, 0, zones_dev, ((scen,),))
        flows = [lax.psum_scatter(whole, "bus", scatter_dimension=0, tiled=True).astype(F32)]

    loadings, worst, at = [], [], 0
    for flow in flows:
        loadings.append(flow / rating[None, at : at + flow.shape[1]])
        worst.append(jnp.max(jnp.abs(loadings[-1]), axis=0))
        at += flow.shape[1]
    worst = max_over_bus(jnp.concatenate(worst), groups)
    return jnp.concatenate(loadings, axis=1), worst


def staged(sites, injections, high, blocks, partial):
    me, here = lax.axis_index("line"), lax.axis_index("bus")
    side = me // 2
    near = here // 4 == side
    by_core = [(i, i ^ 1) for i in range(4)]
    by_y = [(i, i ^ 2) for i in range(4)]
    swap_x = [(i, i ^ 1) for i in range(8)]
    swap_z = [(i, i ^ 2) for i in range(8)]
    swap_far = [(i, i ^ 4) for i in range(8)]

    def to_side(half):
        pairs = []
        for line in range(4):
            goal = (line // 2) ^ half
            pairs += [(line * 8 + b, line * 8 + (b ^ 4)) for b in range(8) if b // 4 != goal]
        return pairs

    def half_injections(half, pieces):
        rows = []
        for q in (3, 1, 2, 0):
            owner = (side ^ half) * 4 + ((here & 3) ^ q)
            rows.append((((owner >> 1) ^ me) & 1) * 2 + (owner & 1))
        return injections(jnp.stack(rows), pieces)

    across = lax.ppermute(sites, "line", by_y)
    other = lax.ppermute(sites, "line", by_core)
    injs = [half_injections(0, [sites, other])]

    zones_dev = blocks.shape[0]
    early = min(EARLY, zones_dev)
    chunks = [((0,), 0, early)] + [((1,), *c) for c in cut(0, early, 2 * STEP)]
    slow = max(early, zones_dev - 2)
    chunks += [((0, 1), *c) for c in cut(early, slow, STEP) + cut(slow, zones_dev, 1)]
    total = len(chunks)
    token = injs[0]
    near_flag = near.astype(jnp.int32).reshape(1)
    splits = ((high, high), (high,), (high,))
    sent, kept, own, moved, late, flows = {}, {}, {}, {}, {}, {}
    for t in range(total + 6):
        stages = [
            (*kept.pop(t - 2), sent.pop(t - 2)) if t - 2 in sent else (),
            (own.pop(t - 4), moved.pop(t - 4)) if t - 4 in moved else (),
            (own.pop(t - 6), late.pop(t - 6)) if t - 6 in late else (),
        ]
        if t < total:
            halves, base, zones = chunks[t]
            if 1 in halves and len(injs) == 1:
                across = copy_after(across, token)
                injs.append(half_injections(1, [across, lax.ppermute(across, "line", by_core)]))
            send, give, keep, *done = partial(
                near_flag,
                token,
                [injs[h] for h in halves],
                blocks,
                base,
                zones,
                splits,
                stages=stages,
            )
            sent[t] = lax.ppermute(send, "bus", swap_x)
            kept[t] = (give, keep)
            token = keep
        else:
            done = sums(near_flag, stages, high)
        done = iter(done)
        if stages[0]:
            moved[t - 2] = lax.ppermute(next(done), "bus", swap_z)
            own[t - 2] = next(done)
        if stages[1]:
            halves = chunks[t - 4][0]
            if len(halves) == 1:
                late[t - 4] = lax.ppermute(next(done), ("line", "bus"), to_side(halves[0]))
            else:
                late[t - 4] = lax.ppermute(next(done), "bus", swap_far)
            own[t - 4] = next(done)
        if stages[2]:
            flows[t - 6] = next(done)
    first_flows = [
        jnp.concatenate([flows[t] for t in range(total) if chunks[t][0] == (half,)], axis=1)
        for half in range(2)
    ]
    flows = [flows[t] for t in range(total) if len(chunks[t][0]) == 2]
    return [jnp.where(near, *first_flows)] + flows


def solution(mesh):
    return jax.shard_map(
        body,
        mesh=mesh,
        in_specs=(
            P("line", "bus"),
            P(),
            P("line", "bus"),
            P("line", "bus"),
            P("line", "bus", None, None),
            P("line"),
        ),
        out_specs=(P("bus", "line"), P("line")),
        check_vma=False,
    )
```

```python
import functools

import jax
import jax.numpy as jnp
from jax import lax
from jax.experimental import pallas as pl
from jax.experimental.pallas import tpu as pltpu
from jax.sharding import PartitionSpec as P

NB = 71680
TILE = 128
WINDOW = 4
EARLY = 8
STEP = 2
Z_FIRST = ()
DEPTH = (3, 2, 2)
F32 = jnp.float32
BF16 = jnp.bfloat16


def params(n, mib=16):
    return pltpu.CompilerParams(
        dimension_semantics=("arbitrary",) * n, vmem_limit_bytes=mib * 1024 * 1024
    )


def cost(flops, nbytes):
    return pl.CostEstimate(flops=int(flops), bytes_accessed=int(nbytes), transcendentals=0)


def hot(ids, first, rows):
    at = lax.broadcasted_iota(jnp.int32, (rows, ids.shape[1]), 0) + first
    return (at == ids).astype(F32).astype(BF16)


def down(row):
    return jnp.broadcast_to(row, (row.shape[1], row.shape[1])).T


def hot_rows(ids, first, columns):
    at = lax.broadcasted_iota(jnp.int32, ids.shape, 1) + first
    tables = [
        (ids == at + c).astype(F32).astype(BF16) for c in range(0, columns, ids.shape[1])
    ]
    return jnp.concatenate(tables, axis=1)


def running_count(mask, part):
    rows, lanes = mask.shape
    mask = mask.astype(F32).astype(BF16)
    up_to = lax.broadcasted_iota(jnp.int32, (lanes, lanes), 0) <= lax.broadcasted_iota(
        jnp.int32, (lanes, lanes), 1
    )
    inside = jnp.dot(mask, up_to.astype(F32).astype(BF16), preferred_element_type=F32)
    r = lax.broadcasted_iota(jnp.int32, (rows, rows), 0)
    c = lax.broadcasted_iota(jnp.int32, (rows, rows), 1)
    earlier = ((c < r) & ((c ^ r) < part)).astype(F32).astype(BF16)
    before = jnp.dot(earlier, mask, preferred_element_type=F32)
    return (inside + jnp.sum(before, axis=1, keepdims=True)).astype(jnp.int32)


def route_kernel(here_ref, bus_ref, values_ref, out_ref, rounded, places, *, groups, bus_dev):
    del here_ref
    group = pl.program_id(0)
    width = out_ref.shape[2]
    rows = bus_ref.shape[0]

    @pl.when(group == 0)
    def _():
        rounded[...] = values_ref[...].astype(BF16)
        ids = bus_ref[...]
        masks = [(ids >= g * bus_dev) & (ids < (g + 1) * bus_dev) for g in range(groups)]
        masks = jnp.concatenate([mask.astype(F32) for mask in masks], axis=0)
        count = running_count(masks, rows)
        place = jnp.zeros(ids.shape, jnp.int32)
        for g in range(groups):
            part = slice(g * rows, (g + 1) * rows)
            place += jnp.where(masks[part] > 0, count[part] + (g * width - 1), 0)
        for r in range(rows):
            places[r * TILE : (r + 1) * TILE] = down(place[r : r + 1])

    total = jnp.zeros(out_ref.shape[1:], F32)
    step = 4 * TILE
    for at in range(0, rows * TILE, step):
        table = hot_rows(places[at : at + step], group * width, width)
        total += jnp.dot(rounded[:, at : at + step], table, preferred_element_type=F32)
    out_ref[0] = total.astype(BF16)


def route(here, site_bus, values, groups, bus_dev):
    scen, depth = values.shape
    width = depth // groups
    rows = depth // TILE
    return pl.pallas_call(
        functools.partial(route_kernel, groups=groups, bus_dev=bus_dev),
        grid_spec=pltpu.PrefetchScalarGridSpec(
            num_scalar_prefetch=1,
            grid=(groups,),
            in_specs=[
                pl.BlockSpec((rows, TILE), lambda g, here: (here[0], 0)),
                pl.BlockSpec((scen, depth), lambda g, here: (0, 0)),
            ],
            out_specs=pl.BlockSpec((1, scen, width), lambda g, here: (g, 0, 0)),
            scratch_shapes=[pltpu.VMEM((scen, depth), BF16), pltpu.VMEM((depth, TILE), jnp.int32)],
        ),
        out_shape=jax.ShapeDtypeStruct((groups, scen, width), BF16),
        compiler_params=params(1),
        cost_estimate=cost(4 * scen * depth * depth, 4 * scen * depth),
        name="route",
    )(here.reshape(1), site_bus.reshape(-1, TILE), values)


def arrivals_kernel(here_ref, bus_ref, out_ref, places, local, *, bus_dev):
    block = pl.program_id(0)
    width = out_ref.shape[2]
    rows = bus_ref.shape[0] // pl.num_programs(0)

    @pl.when(block == 0)
    def _():
        ids = bus_ref[...] - here_ref[0] * bus_dev
        mask = (ids >= 0) & (ids < bus_dev)
        places[...] = jnp.where(mask, running_count(mask, rows) - 1, -1)
        local[...] = jnp.where(mask, ids, 0)

    sub = lax.broadcasted_iota(jnp.int32, (16, TILE), 0)
    total = jnp.zeros((16, width), F32)
    step = 4
    for at in range(0, rows, step):
        tables, parts = [], []
        for r in range(at, at + step):
            row = pl.ds(block * rows + r, 1)
            tables.append(hot_rows(down(places[row]), 0, width))
            ids = local[row]
            part = jnp.where(sub == 0, ids >> 7, jnp.where(sub == 1, ids & 127, 0))
            parts.append(part.astype(F32).astype(BF16))
        total += jnp.dot(
            jnp.concatenate(parts, axis=1),
            jnp.concatenate(tables, axis=0),
            preferred_element_type=F32,
        )
    out_ref[0] = (total[0:1] * 128.0 + total[1:2]).astype(jnp.int32)


def arrivals(here, site_bus, groups, site_dev, bus_dev):
    width = site_dev // groups
    rows = site_bus.shape[0] // TILE
    return pl.pallas_call(
        functools.partial(arrivals_kernel, bus_dev=bus_dev),
        grid_spec=pltpu.PrefetchScalarGridSpec(
            num_scalar_prefetch=1,
            grid=(groups,),
            in_specs=[pl.BlockSpec((rows, TILE), lambda g, here: (0, 0))],
            out_specs=pl.BlockSpec((1, 1, width), lambda g, here: (g, 0, 0)),
            scratch_shapes=[pltpu.VMEM((rows, TILE), jnp.int32)] * 2,
        ),
        out_shape=jax.ShapeDtypeStruct((groups, 1, width), jnp.int32),
        compiler_params=params(1),
        cost_estimate=cost(4 * 16 * site_dev * site_dev, 4 * rows * TILE),
        name="arrivals",
    )(here.reshape(1), site_bus.reshape(-1, TILE))


def merge_kernel(order_ref, runs_ref, out_ref):
    runs, rows, width = runs_ref.shape
    ids = order_ref[0]
    total = jnp.zeros((rows, ids.shape[1]), F32)
    for run in range(runs):
        total += jnp.dot(runs_ref[run], hot(ids, run * width, width), preferred_element_type=F32)
    total = total.astype(BF16)
    for part in range(out_ref.shape[0]):
        out_ref[part] = total[:, part * TILE : (part + 1) * TILE]


def merge(order, runs):
    count, rows, width = runs.shape
    sites = count * width
    step = 4 * TILE
    return pl.pallas_call(
        merge_kernel,
        grid=(sites // step,),
        in_specs=[
            pl.BlockSpec((1, 1, step), lambda t: (t, 0, 0)),
            pl.BlockSpec((count, rows, width), lambda t: (0, 0, 0)),
        ],
        out_specs=pl.BlockSpec((step // TILE, rows, TILE), lambda t: (t, 0, 0)),
        out_shape=jax.ShapeDtypeStruct((sites // TILE, rows, TILE), BF16),
        compiler_params=params(1),
        cost_estimate=cost(4 * rows * sites * sites, 4 * rows * sites),
        name="merge",
    )(order.reshape(sites // step, 1, step), runs)


def inject_kernel(first_ref, windows_ref, rows_ref, ids_ref, *refs):
    pieces, out_ref, total, places = refs[:-3], refs[-3], refs[-2], refs[-1]
    zone = pl.program_id(0)
    scen, width = total.shape
    tiles = ids_ref.shape[0]

    @pl.when(zone == 0)
    def _():
        for t in range(tiles):
            places[t] = down(ids_ref[t])

    def window(w):
        parts, tables = [], []
        for j in range(WINDOW):
            t = first_ref[zone] + w * WINDOW + j
            at = jnp.minimum(t, tiles - 1)
            ids = jnp.where(t < tiles, places[at], -1)
            tables.append(hot_rows(ids, zone * width, width))
            parts.append(jnp.concatenate([piece[at] for piece in pieces], axis=0))
        return jnp.dot(
            jnp.concatenate(parts, axis=1),
            jnp.concatenate(tables, axis=0),
            preferred_element_type=F32,
        )

    total[...] = window(0)

    @pl.loop(1, windows_ref[zone])
    def _(w):
        total[...] += window(w)

    blocks = rows_ref.shape[0]
    high = scen // blocks
    for j in range(blocks):
        rows = pl.ds(pl.multiple_of(rows_ref[j] * high, high), high)
        out_ref[0, j * high : (j + 1) * high] = total[rows, :].astype(BF16)


def inject(first, windows, row_blocks, ids, pieces, zones, width):
    tiles, rows, _ = pieces[0].shape
    scen = rows * len(pieces)
    whole = pl.BlockSpec((tiles, rows, TILE), lambda z, *_: (0, 0, 0))
    return pl.pallas_call(
        inject_kernel,
        grid_spec=pltpu.PrefetchScalarGridSpec(
            num_scalar_prefetch=3,
            grid=(zones,),
            in_specs=[pl.BlockSpec((tiles, 1, TILE), lambda z, *_: (0, 0, 0))]
            + [whole] * len(pieces),
            out_specs=pl.BlockSpec((1, scen, width), lambda z, *_: (z, 0, 0)),
            scratch_shapes=[
                pltpu.VMEM((scen, width), F32),
                pltpu.VMEM((tiles, TILE, TILE), jnp.int32),
            ],
        ),
        out_shape=jax.ShapeDtypeStruct((zones, scen, width), BF16),
        compiler_params=params(1),
        cost_estimate=cost(1 << 16, 1 << 10),
        name="inject",
    )(first, windows, row_blocks, ids, *pieces)


def sum_x(give, own, received):
    rows = give.shape[0]
    return (
        add(give[...], received[:rows]).astype(BF16),
        add(own[...], received[rows:]).astype(BF16),
    )


def sum_z(own, received, near, high):
    mine = add(own[...], received[...]).astype(BF16)
    if mine.shape[0] == high:
        return mine, mine
    low, top = mine[:high], mine[high:]
    return jnp.where(near, top, low), jnp.where(near, low, top)


def run_stages(taken, outs, near, high):
    if taken[0]:
        for result in sum_x(*taken[0]):
            next(outs)[...] = result
    if taken[1]:
        for result in sum_z(*taken[1], near, high):
            next(outs)[...] = result
    if taken[2]:
        next(outs)[...] = add(taken[2][0][...], taken[2][1][...])


def stage_shapes(stages, high):
    shapes = [jax.ShapeDtypeStruct(array.shape, BF16) for array in stages[0][:2]]
    shapes += [jax.ShapeDtypeStruct((high, array.shape[1]), BF16) for array in stages[1]]
    return shapes + [jax.ShapeDtypeStruct(array.shape, F32) for array in stages[2][:1]]


def sums_kernel(near_ref, *refs, stages, high):
    extra = iter(refs)
    taken = [[next(extra) for _ in range(count)] for count in stages]
    run_stages(taken, extra, near_ref[0] == 1, high)


def sums(near, stages, high):
    vmem = pl.BlockSpec(memory_space=pltpu.VMEM)
    shapes = stage_shapes(stages, high)
    return pl.pallas_call(
        functools.partial(sums_kernel, stages=[len(stage) for stage in stages], high=high),
        in_specs=[pl.BlockSpec(memory_space=pltpu.SMEM)] + [vmem] * sum(map(len, stages)),
        out_specs=[vmem] * len(shapes),
        out_shape=shapes,
        compiler_params=pltpu.CompilerParams(vmem_limit_bytes=32 * 1024 * 1024),
        cost_estimate=cost(1 << 16, 1 << 10),
        name="sums",
    )(near, *[array for stage in stages for array in stage])


def flow_kernel(
    count_ref, zone_ref, last_ref, near_ref, token_ref, *refs, base, slots, halves, splits, stages
):
    inj, blocks = refs[: halves * slots], refs[halves * slots : (halves + 1) * slots]
    extra = iter(refs[(halves + 1) * slots :])
    taken = [[next(extra) for _ in range(count)] for count in stages]
    outs = [next(extra) for _ in splits]

    if any(stages):

        @pl.when(pl.program_id(0) == 0)
        def _():
            run_stages(taken, extra, near_ref[0] == 1, splits[-1][-1][1])

    live = count_ref[pl.program_id(0) + base]
    for count in range(slots + 1):

        @pl.when(live == count)
        def _(count=count):
            if count == 0:
                for out in outs:
                    out[...] = jnp.zeros_like(out)
                return
            for half in range(halves):
                total = sum(
                    lax.dot_general(
                        inj[half * slots + k][0],
                        blocks[k][0, 0],
                        (((1,), (1,)), ((), ())),
                        preferred_element_type=F32,
                    )
                    for k in range(count)
                )
                for out, parts in zip(outs, splits):
                    for i, (row, rows) in enumerate(parts):
                        at = (i * halves + half) * rows
                        out[at : at + rows] = total[row : row + rows].astype(BF16)


def last_live(count, slots):
    zones = count.shape[0]
    at = jnp.arange(zones, dtype=jnp.int32)[:, None]
    live = jnp.arange(slots, dtype=jnp.int32)[None, :] < count[:, None]
    return lax.cummax(jnp.where(live, at, 0), axis=0).reshape(-1)


def partial_flow(
    count, zone, last, near, token, injs, blocks, base, zones, splits, stages=((), (), ())
):
    _, slots, lines, width = blocks.shape
    scen = injs[0].shape[1]
    halves = len(injs)

    def inj_at(k):
        def at(z, count, zone, last, near):
            return zone[last[(z + base) * slots + k] * slots + k], 0, 0

        return pl.BlockSpec((1, scen, width), at)

    def block_at(k):
        def at(z, count, zone, last, near):
            return last[(z + base) * slots + k], k, 0, 0

        return pl.BlockSpec((1, 1, lines, width), at)

    def whole(array):
        return pl.BlockSpec(array.shape, lambda z, *_: (0, 0))

    high = splits[-1][-1][1]
    shapes = [
        jax.ShapeDtypeStruct((halves * len(parts) * parts[0][1], zones * lines), BF16)
        for parts in splits
    ]
    later = stage_shapes(stages, high)
    extra = [array for stage in stages for array in stage]
    live = zones * slots / 2
    return pl.pallas_call(
        functools.partial(
            flow_kernel,
            base=base,
            slots=slots,
            halves=halves,
            splits=splits,
            stages=[len(stage) for stage in stages],
        ),
        grid_spec=pltpu.PrefetchScalarGridSpec(
            num_scalar_prefetch=4,
            grid=(zones,),
            in_specs=[pl.BlockSpec(memory_space=pl.ANY)]
            + [inj_at(k) for k in range(slots)] * halves
            + [block_at(k) for k in range(slots)]
            + [whole(array) for array in extra],
            out_specs=[
                pl.BlockSpec((halves * len(parts) * parts[0][1], lines), lambda z, *_: (0, z))
                for parts in splits
            ]
            + [whole(array) for array in later],
        ),
        out_shape=shapes + later,
        compiler_params=params(1, 32),
        cost_estimate=cost(
            2 * live * halves * scen * lines * width, 2 * live * (halves * scen + lines) * width
        ),
        name="partial_flow",
    )(
        count,
        zone,
        last,
        near,
        token,
        *[inj for inj in injs for _ in range(slots)],
        *[blocks] * slots,
        *extra,
    )


def copy_after(values, token):
    def kernel(values_ref, token_ref, out_ref):
        out_ref[...] = values_ref[...]

    tiles, rows, lanes = values.shape
    block = pl.BlockSpec((tiles // 4, rows, lanes), lambda i: (i, 0, 0))
    return pl.pallas_call(
        kernel,
        grid=(4,),
        in_specs=[block, pl.BlockSpec(memory_space=pl.ANY)],
        out_specs=block,
        out_shape=jax.ShapeDtypeStruct(values.shape, values.dtype),
        compiler_params=params(1),
        cost_estimate=cost(1 << 16, 1 << 10),
        name="copy_after",
    )(values, token)


def cut(first, last, size):
    return [(base, min(size, last - base)) for base in range(first, last, size)]


def add(*terms):
    return sum(term.astype(F32) for term in terms)


def max_over_bus(values, groups):
    if groups & (groups - 1):
        return lax.pmax(values, "bus")
    for steps in ((1,), range(2, groups, 2)):
        others = [
            lax.ppermute(values, "bus", [(i, i ^ step) for i in range(groups)]) for step in steps
        ]
        values = functools.reduce(jnp.maximum, others, values)
    return values


def body(site_values, site_bus, block_count, block_zone, ptdf_blocks, rating):
    here = lax.axis_index("bus")
    groups = lax.axis_size("bus")
    lines_size = lax.axis_size("line")
    scen_part, site_dev = site_values.shape
    bus_dev = NB // groups
    group_sites = groups * (site_dev // groups)
    zones_dev, slots_dev, line_zone, zone_width = ptdf_blocks.shape
    bus_zones = bus_dev // zone_width
    scen = scen_part * lines_size
    high = scen // groups

    got = lax.all_to_all(
        route(here, site_bus, site_values, groups, bus_dev), "bus", 0, 0, tiled=True
    )

    local = arrivals(here, site_bus, groups, site_dev, bus_dev).reshape(group_sites)
    keys = lax.sort(local * group_sites + jnp.arange(group_sites, dtype=jnp.int32))
    local = keys // group_sites
    edges = jnp.arange(bus_zones + 1, dtype=jnp.int32) * zone_width
    starts = jnp.sum((local[None, :] < edges[:, None]).astype(jnp.int32), axis=1)
    first = starts[:-1] // TILE
    span = WINDOW * TILE
    windows = (starts[1:] - first * TILE + span - 1) // span
    ids = local.reshape(group_sites // TILE, 1, TILE)
    count = block_count[:, 0]
    zone = block_zone.reshape(-1)
    last = last_live(count, slots_dev)
    sites = merge(keys % group_sites, got)

    def injections(row_blocks, pieces):
        return inject(
            first, windows, row_blocks.astype(jnp.int32), ids, pieces, bus_zones, zone_width
        )

    def partial(*call, **options):
        return partial_flow(count, zone, last, *call, **options)

    if groups == 8 and lines_size == 4 and scen_part == 2 * high:
        flows = staged(sites, injections, high, ptdf_blocks, partial)
    else:
        gathered = lax.all_gather(sites, "line", axis=0)
        inj = injections(jnp.arange(groups), [gathered[i] for i in range(lines_size)])
        (whole,) = partial(here.reshape(1), count, [inj], ptdf_blocks, 0, zones_dev, (((0, scen),),))
        flows = [lax.psum_scatter(whole, "bus", scatter_dimension=0, tiled=True).astype(F32)]

    loadings, worst, at = [], [], 0
    for flow in flows:
        loadings.append(flow / rating[None, at : at + flow.shape[1]])
        worst.append(jnp.max(jnp.abs(loadings[-1]), axis=0))
        at += flow.shape[1]
    worst = max_over_bus(jnp.concatenate(worst), groups)
    return jnp.concatenate(loadings, axis=1), worst


def staged(sites, injections, high, blocks, partial):
    me, here = lax.axis_index("line"), lax.axis_index("bus")
    side = me // 2
    near = here // 4 == side
    by_core = [(i, i ^ 1) for i in range(4)]
    by_y = [(i, i ^ 2) for i in range(4)]
    swap_x = [(i, i ^ 1) for i in range(8)]
    swap_z = [(i, i ^ 2) for i in range(8)]
    swap_far = [(i, i ^ 4) for i in range(8)]

    def to_side(half):
        pairs = []
        for line in range(4):
            goal = (line // 2) ^ half
            pairs += [(line * 8 + b, line * 8 + (b ^ 4)) for b in range(8) if b // 4 != goal]
        return pairs

    def half_injections(half, pieces):
        rows = []
        for q in (3, 1, 2, 0):
            owner = (side ^ half) * 4 + ((here & 3) ^ q)
            rows.append((((owner >> 1) ^ me) & 1) * 2 + (owner & 1))
        return injections(jnp.stack(rows), pieces)

    across = lax.ppermute(sites, "line", by_y)
    other = lax.ppermute(sites, "line", by_core)
    injs = [half_injections(0, [sites, other])]

    zones_dev = blocks.shape[0]
    early = min(EARLY, zones_dev)
    chunks = [((0,), *c) for c in cut(0, early, 4)] + [((1,), *c) for c in cut(0, early, 2 * STEP)]
    slow = max(early, zones_dev - 2)
    chunks += [((0, 1), *c) for c in cut(early, slow, STEP) + cut(slow, zones_dev, 1)]
    total = len(chunks)
    token = injs[0]
    near_flag = near.astype(jnp.int32).reshape(1)
    row = {q: (i * high, high) for i, q in enumerate((3, 1, 2, 0))}
    full = [t for t in range(total) if len(chunks[t][0]) == 2]
    z_first = [full[i] for i in Z_FIRST if i < len(full)]
    swaps = [(swap_z, swap_x) if t in z_first else (swap_x, swap_z) for t in range(total)]
    sent, kept, own, moved, late, flows, ending = {}, {}, {}, {}, {}, {}, {}
    summed, shared, ended = DEPTH[0], sum(DEPTH[:2]), sum(DEPTH)
    for t in range(total + ended):
        stages = [
            (*kept.pop(t - summed), sent.pop(t - summed)) if t - summed in sent else (),
            (own.pop(t - shared), moved.pop(t - shared)) if t - shared in moved else (),
            (own.pop(t - ended), late.pop(t - ended)) if t - ended in late else (),
        ]
        if t < total:
            halves, base, zones = chunks[t]
            if 1 in halves and len(injs) == 1:
                across = copy_after(across, token)
                injs.append(half_injections(1, [across, lax.ppermute(across, "line", by_core)]))
            lead, then = (2, 1) if t in z_first else (1, 2)
            splits = ((row[3], row[lead]), (row[then],), (row[0],))
            send, give, keep, *done = partial(
                near_flag,
                token,
                [injs[h] for h in halves],
                blocks,
                base,
                zones,
                splits,
                stages=stages,
            )
            sent[t] = lax.ppermute(send, "bus", swaps[t][0])
            kept[t] = (give, keep)
            token = keep
        else:
            ending[t - ended], stages[2] = stages[2], ()
            done = sums(near_flag, stages, high) if any(stages) else []
        done = iter(done)
        if stages[0]:
            moved[t - summed] = lax.ppermute(next(done), "bus", swaps[t - summed][1])
            own[t - summed] = next(done)
        if stages[1]:
            halves = chunks[t - shared][0]
            if len(halves) == 1:
                late[t - shared] = lax.ppermute(next(done), ("line", "bus"), to_side(halves[0]))
            else:
                late[t - shared] = lax.ppermute(next(done), "bus", swap_far)
            own[t - shared] = next(done)
        if stages[2]:
            flows[t - ended] = next(done)
    flows.update((t, add(*stage)) for t, stage in ending.items() if stage)
    first_flows = [
        jnp.concatenate([flows[t] for t in range(total) if chunks[t][0] == (half,)], axis=1)
        for half in range(2)
    ]
    flows = [flows[t] for t in range(total) if len(chunks[t][0]) == 2]
    return [jnp.where(near, *first_flows)] + flows


def solution(mesh):
    return jax.shard_map(
        body,
        mesh=mesh,
        in_specs=(
            P("line", "bus"),
            P(),
            P("line", "bus"),
            P("line", "bus"),
            P("line", "bus", None, None),
            P("line"),
        ),
        out_specs=(P("bus", "line"), P("line")),
        check_vma=False,
    )
```

```python
import functools

import jax
import jax.numpy as jnp
from jax import lax
from jax.experimental import pallas as pl
from jax.experimental.pallas import tpu as pltpu
from jax.sharding import PartitionSpec as P

NB = 71680
TILE = 128
WINDOW = 4
EARLY = 8
STEP = 2
Z_FIRST = ()
DEPTH = (3, 2, 2)
F32 = jnp.float32
BF16 = jnp.bfloat16


def params(n, mib=16):
    return pltpu.CompilerParams(
        dimension_semantics=("arbitrary",) * n, vmem_limit_bytes=mib * 1024 * 1024
    )


def cost(flops, nbytes):
    return pl.CostEstimate(flops=int(flops), bytes_accessed=int(nbytes), transcendentals=0)


def hot(ids, first, rows):
    at = lax.broadcasted_iota(jnp.int32, (rows, ids.shape[1]), 0) + first
    return (at == ids).astype(F32).astype(BF16)


def down(row):
    return jnp.broadcast_to(row, (row.shape[1], row.shape[1])).T


def hot_rows(ids, first, columns):
    at = lax.broadcasted_iota(jnp.int32, ids.shape, 1) + first
    tables = [
        (ids == at + c).astype(F32).astype(BF16) for c in range(0, columns, ids.shape[1])
    ]
    return jnp.concatenate(tables, axis=1)


def running_count(mask, part):
    rows, lanes = mask.shape
    mask = mask.astype(F32).astype(BF16)
    up_to = lax.broadcasted_iota(jnp.int32, (lanes, lanes), 0) <= lax.broadcasted_iota(
        jnp.int32, (lanes, lanes), 1
    )
    inside = jnp.dot(mask, up_to.astype(F32).astype(BF16), preferred_element_type=F32)
    r = lax.broadcasted_iota(jnp.int32, (rows, rows), 0)
    c = lax.broadcasted_iota(jnp.int32, (rows, rows), 1)
    earlier = ((c < r) & ((c ^ r) < part)).astype(F32).astype(BF16)
    before = jnp.dot(earlier, mask, preferred_element_type=F32)
    return (inside + jnp.sum(before, axis=1, keepdims=True)).astype(jnp.int32)


def route_kernel(here_ref, bus_ref, values_ref, out_ref, rounded, places, *, groups, bus_dev):
    del here_ref
    group = pl.program_id(0)
    width = out_ref.shape[2]
    rows = bus_ref.shape[0]

    @pl.when(group == 0)
    def _():
        rounded[...] = values_ref[...].astype(BF16)
        ids = bus_ref[...]
        masks = [(ids >= g * bus_dev) & (ids < (g + 1) * bus_dev) for g in range(groups)]
        masks = jnp.concatenate([mask.astype(F32) for mask in masks], axis=0)
        count = running_count(masks, rows)
        place = jnp.zeros(ids.shape, jnp.int32)
        for g in range(groups):
            part = slice(g * rows, (g + 1) * rows)
            place += jnp.where(masks[part] > 0, count[part] + (g * width - 1), 0)
        for r in range(rows):
            places[r * TILE : (r + 1) * TILE] = down(place[r : r + 1])

    total = jnp.zeros(out_ref.shape[1:], F32)
    step = 4 * TILE
    for at in range(0, rows * TILE, step):
        table = hot_rows(places[at : at + step], group * width, width)
        total += jnp.dot(rounded[:, at : at + step], table, preferred_element_type=F32)
    out_ref[0] = total.astype(BF16)


def route(here, site_bus, values, groups, bus_dev):
    scen, depth = values.shape
    width = depth // groups
    rows = depth // TILE
    return pl.pallas_call(
        functools.partial(route_kernel, groups=groups, bus_dev=bus_dev),
        grid_spec=pltpu.PrefetchScalarGridSpec(
            num_scalar_prefetch=1,
            grid=(groups,),
            in_specs=[
                pl.BlockSpec((rows, TILE), lambda g, here: (here[0], 0)),
                pl.BlockSpec((scen, depth), lambda g, here: (0, 0)),
            ],
            out_specs=pl.BlockSpec((1, scen, width), lambda g, here: (g, 0, 0)),
            scratch_shapes=[pltpu.VMEM((scen, depth), BF16), pltpu.VMEM((depth, TILE), jnp.int32)],
        ),
        out_shape=jax.ShapeDtypeStruct((groups, scen, width), BF16),
        compiler_params=params(1),
        cost_estimate=cost(4 * scen * depth * depth, 4 * scen * depth),
        name="route",
    )(here.reshape(1), site_bus.reshape(-1, TILE), values)


def arrivals_kernel(here_ref, bus_ref, out_ref, places, local, *, bus_dev):
    block = pl.program_id(0)
    width = out_ref.shape[2]
    rows = bus_ref.shape[0] // pl.num_programs(0)

    @pl.when(block == 0)
    def _():
        ids = bus_ref[...] - here_ref[0] * bus_dev
        mask = (ids >= 0) & (ids < bus_dev)
        places[...] = jnp.where(mask, running_count(mask, rows) - 1, -1)
        local[...] = jnp.where(mask, ids, 0)

    sub = lax.broadcasted_iota(jnp.int32, (16, TILE), 0)
    total = jnp.zeros((16, width), F32)
    step = 4
    for at in range(0, rows, step):
        tables, parts = [], []
        for r in range(at, at + step):
            row = pl.ds(block * rows + r, 1)
            tables.append(hot_rows(down(places[row]), 0, width))
            ids = local[row]
            part = jnp.where(sub == 0, ids >> 7, jnp.where(sub == 1, ids & 127, 0))
            parts.append(part.astype(F32).astype(BF16))
        total += jnp.dot(
            jnp.concatenate(parts, axis=1),
            jnp.concatenate(tables, axis=0),
            preferred_element_type=F32,
        )
    out_ref[0] = (total[0:1] * 128.0 + total[1:2]).astype(jnp.int32)


def arrivals(here, site_bus, groups, site_dev, bus_dev):
    width = site_dev // groups
    rows = site_bus.shape[0] // TILE
    return pl.pallas_call(
        functools.partial(arrivals_kernel, bus_dev=bus_dev),
        grid_spec=pltpu.PrefetchScalarGridSpec(
            num_scalar_prefetch=1,
            grid=(groups,),
            in_specs=[pl.BlockSpec((rows, TILE), lambda g, here: (0, 0))],
            out_specs=pl.BlockSpec((1, 1, width), lambda g, here: (g, 0, 0)),
            scratch_shapes=[pltpu.VMEM((rows, TILE), jnp.int32)] * 2,
        ),
        out_shape=jax.ShapeDtypeStruct((groups, 1, width), jnp.int32),
        compiler_params=params(1),
        cost_estimate=cost(4 * 16 * site_dev * site_dev, 4 * rows * TILE),
        name="arrivals",
    )(here.reshape(1), site_bus.reshape(-1, TILE))


def merge_kernel(order_ref, runs_ref, out_ref):
    runs, rows, width = runs_ref.shape
    ids = order_ref[0]
    total = jnp.zeros((rows, ids.shape[1]), F32)
    for run in range(runs):
        total += jnp.dot(runs_ref[run], hot(ids, run * width, width), preferred_element_type=F32)
    total = total.astype(BF16)
    for part in range(out_ref.shape[0]):
        out_ref[part] = total[:, part * TILE : (part + 1) * TILE]


def merge(order, runs):
    count, rows, width = runs.shape
    sites = count * width
    step = 4 * TILE
    return pl.pallas_call(
        merge_kernel,
        grid=(sites // step,),
        in_specs=[
            pl.BlockSpec((1, 1, step), lambda t: (t, 0, 0)),
            pl.BlockSpec((count, rows, width), lambda t: (0, 0, 0)),
        ],
        out_specs=pl.BlockSpec((step // TILE, rows, TILE), lambda t: (t, 0, 0)),
        out_shape=jax.ShapeDtypeStruct((sites // TILE, rows, TILE), BF16),
        compiler_params=params(1),
        cost_estimate=cost(4 * rows * sites * sites, 4 * rows * sites),
        name="merge",
    )(order.reshape(sites // step, 1, step), runs)


def inject_kernel(first_ref, windows_ref, rows_ref, ids_ref, *refs):
    pieces, out_ref, total, places = refs[:-3], refs[-3], refs[-2], refs[-1]
    zone = pl.program_id(0)
    scen, width = total.shape
    tiles = ids_ref.shape[0]

    @pl.when(zone == 0)
    def _():
        for t in range(tiles):
            places[t] = down(ids_ref[t])

    def window(w):
        parts, tables = [], []
        for j in range(WINDOW):
            t = first_ref[zone] + w * WINDOW + j
            at = jnp.minimum(t, tiles - 1)
            ids = jnp.where(t < tiles, places[at], -1)
            tables.append(hot_rows(ids, zone * width, width))
            parts.append(jnp.concatenate([piece[at] for piece in pieces], axis=0))
        return jnp.dot(
            jnp.concatenate(parts, axis=1),
            jnp.concatenate(tables, axis=0),
            preferred_element_type=F32,
        )

    total[...] = window(0)

    @pl.loop(1, windows_ref[zone])
    def _(w):
        total[...] += window(w)

    blocks = rows_ref.shape[0]
    high = scen // blocks
    for j in range(blocks):
        rows = pl.ds(pl.multiple_of(rows_ref[j] * high, high), high)
        out_ref[0, j * high : (j + 1) * high] = total[rows, :].astype(BF16)


def inject(first, windows, row_blocks, ids, pieces, zones, width):
    tiles, rows, _ = pieces[0].shape
    scen = rows * len(pieces)
    whole = pl.BlockSpec((tiles, rows, TILE), lambda z, *_: (0, 0, 0))
    return pl.pallas_call(
        inject_kernel,
        grid_spec=pltpu.PrefetchScalarGridSpec(
            num_scalar_prefetch=3,
            grid=(zones,),
            in_specs=[pl.BlockSpec((tiles, 1, TILE), lambda z, *_: (0, 0, 0))]
            + [whole] * len(pieces),
            out_specs=pl.BlockSpec((1, scen, width), lambda z, *_: (z, 0, 0)),
            scratch_shapes=[
                pltpu.VMEM((scen, width), F32),
                pltpu.VMEM((tiles, TILE, TILE), jnp.int32),
            ],
        ),
        out_shape=jax.ShapeDtypeStruct((zones, scen, width), BF16),
        compiler_params=params(1),
        cost_estimate=cost(1 << 16, 1 << 10),
        name="inject",
    )(first, windows, row_blocks, ids, *pieces)


def sum_x(give, own, received):
    rows = give.shape[0]
    return (
        add(give[...], received[:rows]).astype(BF16),
        add(own[...], received[rows:]).astype(BF16),
    )


def sum_z(own, received, near, high):
    mine = add(own[...], received[...]).astype(BF16)
    if mine.shape[0] == high:
        return mine, mine
    low, top = mine[:high], mine[high:]
    return jnp.where(near, top, low), jnp.where(near, low, top)


def run_stages(taken, outs, near, high):
    if taken[0]:
        for result in sum_x(*taken[0]):
            next(outs)[...] = result
    if taken[1]:
        for result in sum_z(*taken[1], near, high):
            next(outs)[...] = result
    if taken[2]:
        next(outs)[...] = add(taken[2][0][...], taken[2][1][...])


def stage_shapes(stages, high):
    shapes = [jax.ShapeDtypeStruct(array.shape, BF16) for array in stages[0][:2]]
    shapes += [jax.ShapeDtypeStruct((high, array.shape[1]), BF16) for array in stages[1]]
    return shapes + [jax.ShapeDtypeStruct(array.shape, F32) for array in stages[2][:1]]


def sums_kernel(near_ref, token_ref, *refs, stages, high):
    extra = iter(refs)
    taken = [[next(extra) for _ in range(count)] for count in stages]
    run_stages(taken, extra, near_ref[0] == 1, high)


def sums(near, token, stages, high):
    vmem = pl.BlockSpec(memory_space=pltpu.VMEM)
    shapes = stage_shapes(stages, high)
    return pl.pallas_call(
        functools.partial(sums_kernel, stages=[len(stage) for stage in stages], high=high),
        in_specs=[pl.BlockSpec(memory_space=pltpu.SMEM), pl.BlockSpec(memory_space=pl.ANY)]
        + [vmem] * sum(map(len, stages)),
        out_specs=[vmem] * len(shapes),
        out_shape=shapes,
        compiler_params=pltpu.CompilerParams(vmem_limit_bytes=32 * 1024 * 1024),
        cost_estimate=cost(1 << 16, 1 << 10),
        name="sums",
    )(near, token, *[array for stage in stages for array in stage])


def flow_kernel(
    count_ref, zone_ref, last_ref, near_ref, token_ref, *refs, base, slots, halves, splits, stages
):
    inj, blocks = refs[: halves * slots], refs[halves * slots : (halves + 1) * slots]
    extra = iter(refs[(halves + 1) * slots :])
    taken = [[next(extra) for _ in range(count)] for count in stages]
    outs = [next(extra) for _ in splits]

    if any(stages):

        @pl.when(pl.program_id(0) == 0)
        def _():
            run_stages(taken, extra, near_ref[0] == 1, splits[-1][-1][1])

    live = count_ref[pl.program_id(0) + base]
    for count in range(slots + 1):

        @pl.when(live == count)
        def _(count=count):
            if count == 0:
                for out in outs:
                    out[...] = jnp.zeros_like(out)
                return
            for half in range(halves):
                total = sum(
                    lax.dot_general(
                        inj[half * slots + k][0],
                        blocks[k][0, 0],
                        (((1,), (1,)), ((), ())),
                        preferred_element_type=F32,
                    )
                    for k in range(count)
                )
                for out, parts in zip(outs, splits):
                    for i, (row, rows) in enumerate(parts):
                        at = (i * halves + half) * rows
                        out[at : at + rows] = total[row : row + rows].astype(BF16)


def last_live(count, slots):
    zones = count.shape[0]
    at = jnp.arange(zones, dtype=jnp.int32)[:, None]
    live = jnp.arange(slots, dtype=jnp.int32)[None, :] < count[:, None]
    return lax.cummax(jnp.where(live, at, 0), axis=0).reshape(-1)


def partial_flow(
    count, zone, last, near, token, injs, blocks, base, zones, splits, stages=((), (), ())
):
    _, slots, lines, width = blocks.shape
    scen = injs[0].shape[1]
    halves = len(injs)

    def inj_at(k):
        def at(z, count, zone, last, near):
            return zone[last[(z + base) * slots + k] * slots + k], 0, 0

        return pl.BlockSpec((1, scen, width), at)

    def block_at(k):
        def at(z, count, zone, last, near):
            return last[(z + base) * slots + k], k, 0, 0

        return pl.BlockSpec((1, 1, lines, width), at)

    def whole(array):
        return pl.BlockSpec(array.shape, lambda z, *_: (0, 0))

    high = splits[-1][-1][1]
    shapes = [
        jax.ShapeDtypeStruct((halves * len(parts) * parts[0][1], zones * lines), BF16)
        for parts in splits
    ]
    later = stage_shapes(stages, high)
    extra = [array for stage in stages for array in stage]
    live = zones * slots / 2
    return pl.pallas_call(
        functools.partial(
            flow_kernel,
            base=base,
            slots=slots,
            halves=halves,
            splits=splits,
            stages=[len(stage) for stage in stages],
        ),
        grid_spec=pltpu.PrefetchScalarGridSpec(
            num_scalar_prefetch=4,
            grid=(zones,),
            in_specs=[pl.BlockSpec(memory_space=pl.ANY)]
            + [inj_at(k) for k in range(slots)] * halves
            + [block_at(k) for k in range(slots)]
            + [whole(array) for array in extra],
            out_specs=[
                pl.BlockSpec((halves * len(parts) * parts[0][1], lines), lambda z, *_: (0, z))
                for parts in splits
            ]
            + [whole(array) for array in later],
        ),
        out_shape=shapes + later,
        compiler_params=params(1, 32),
        cost_estimate=cost(
            2 * live * halves * scen * lines * width, 2 * live * (halves * scen + lines) * width
        ),
        name="partial_flow",
    )(
        count,
        zone,
        last,
        near,
        token,
        *[inj for inj in injs for _ in range(slots)],
        *[blocks] * slots,
        *extra,
    )


def copy_after(values, token):
    def kernel(values_ref, token_ref, out_ref):
        out_ref[...] = values_ref[...]

    tiles, rows, lanes = values.shape
    block = pl.BlockSpec((tiles // 4, rows, lanes), lambda i: (i, 0, 0))
    return pl.pallas_call(
        kernel,
        grid=(4,),
        in_specs=[block, pl.BlockSpec(memory_space=pl.ANY)],
        out_specs=block,
        out_shape=jax.ShapeDtypeStruct(values.shape, values.dtype),
        compiler_params=params(1),
        cost_estimate=cost(1 << 16, 1 << 10),
        name="copy_after",
    )(values, token)


def cut(first, last, size):
    return [(base, min(size, last - base)) for base in range(first, last, size)]


def add(*terms):
    return sum(term.astype(F32) for term in terms)


def max_over_bus(values, groups):
    if groups & (groups - 1):
        return lax.pmax(values, "bus")
    for steps in ((1,), range(2, groups, 2)):
        others = [
            lax.ppermute(values, "bus", [(i, i ^ step) for i in range(groups)]) for step in steps
        ]
        values = functools.reduce(jnp.maximum, others, values)
    return values


def body(site_values, site_bus, block_count, block_zone, ptdf_blocks, rating):
    here = lax.axis_index("bus")
    groups = lax.axis_size("bus")
    lines_size = lax.axis_size("line")
    scen_part, site_dev = site_values.shape
    bus_dev = NB // groups
    group_sites = groups * (site_dev // groups)
    zones_dev, slots_dev, line_zone, zone_width = ptdf_blocks.shape
    bus_zones = bus_dev // zone_width
    scen = scen_part * lines_size
    high = scen // groups

    got = lax.all_to_all(
        route(here, site_bus, site_values, groups, bus_dev), "bus", 0, 0, tiled=True
    )

    local = arrivals(here, site_bus, groups, site_dev, bus_dev).reshape(group_sites)
    keys = lax.sort(local * group_sites + jnp.arange(group_sites, dtype=jnp.int32))
    local = keys // group_sites
    edges = jnp.arange(bus_zones + 1, dtype=jnp.int32) * zone_width
    starts = jnp.sum((local[None, :] < edges[:, None]).astype(jnp.int32), axis=1)
    first = starts[:-1] // TILE
    span = WINDOW * TILE
    windows = (starts[1:] - first * TILE + span - 1) // span
    ids = local.reshape(group_sites // TILE, 1, TILE)
    count = block_count[:, 0]
    zone = block_zone.reshape(-1)
    last = last_live(count, slots_dev)
    sites = merge(keys % group_sites, got)

    def injections(row_blocks, pieces):
        return inject(
            first, windows, row_blocks.astype(jnp.int32), ids, pieces, bus_zones, zone_width
        )

    def partial(*call, **options):
        return partial_flow(count, zone, last, *call, **options)

    if groups == 8 and lines_size == 4 and scen_part == 2 * high:
        flows = staged(sites, injections, high, ptdf_blocks, partial)
    else:
        gathered = lax.all_gather(sites, "line", axis=0)
        inj = injections(jnp.arange(groups), [gathered[i] for i in range(lines_size)])
        (whole,) = partial(here.reshape(1), count, [inj], ptdf_blocks, 0, zones_dev, (((0, scen),),))
        flows = [lax.psum_scatter(whole, "bus", scatter_dimension=0, tiled=True).astype(F32)]

    loadings, worst, at = [], [], 0
    for flow in flows:
        loadings.append(flow / rating[None, at : at + flow.shape[1]])
        worst.append(jnp.max(jnp.abs(loadings[-1]), axis=0))
        at += flow.shape[1]
    worst = max_over_bus(jnp.concatenate(worst), groups)
    return jnp.concatenate(loadings, axis=1), worst


def staged(sites, injections, high, blocks, partial):
    me, here = lax.axis_index("line"), lax.axis_index("bus")
    side = me // 2
    near = here // 4 == side
    by_core = [(i, i ^ 1) for i in range(4)]
    by_y = [(i, i ^ 2) for i in range(4)]
    swap_x = [(i, i ^ 1) for i in range(8)]
    swap_z = [(i, i ^ 2) for i in range(8)]
    swap_far = [(i, i ^ 4) for i in range(8)]

    def to_side(half):
        pairs = []
        for line in range(4):
            goal = (line // 2) ^ half
            pairs += [(line * 8 + b, line * 8 + (b ^ 4)) for b in range(8) if b // 4 != goal]
        return pairs

    def half_injections(half, pieces):
        rows = []
        for q in (3, 1, 2, 0):
            owner = (side ^ half) * 4 + ((here & 3) ^ q)
            rows.append((((owner >> 1) ^ me) & 1) * 2 + (owner & 1))
        return injections(jnp.stack(rows), pieces)

    across = lax.ppermute(sites, "line", by_y)
    other = lax.ppermute(sites, "line", by_core)
    injs = [half_injections(0, [sites, other])]

    zones_dev = blocks.shape[0]
    early = min(EARLY, zones_dev)
    chunks = [((0,), *c) for c in cut(0, early, 4)] + [((1,), *c) for c in cut(0, early, 2 * STEP)]
    slow = max(early, zones_dev - 2)
    chunks += [((0, 1), *c) for c in cut(early, slow, STEP) + cut(slow, zones_dev, 1)]
    total = len(chunks)
    token = injs[0]
    near_flag = near.astype(jnp.int32).reshape(1)
    row = {q: (i * high, high) for i, q in enumerate((3, 1, 2, 0))}
    full = [t for t in range(total) if len(chunks[t][0]) == 2]
    z_first = [full[i] for i in Z_FIRST if i < len(full)]
    swaps = [(swap_z, swap_x) if t in z_first else (swap_x, swap_z) for t in range(total)]
    sent, kept, own, moved, late, flows, ending = {}, {}, {}, {}, {}, {}, {}
    summed, shared, ended = DEPTH[0], sum(DEPTH[:2]), sum(DEPTH)
    for t in range(total + ended):
        stages = [
            (*kept.pop(t - summed), sent.pop(t - summed)) if t - summed in sent else (),
            (own.pop(t - shared), moved.pop(t - shared)) if t - shared in moved else (),
            (own.pop(t - ended), late.pop(t - ended)) if t - ended in late else (),
        ]
        if t < total:
            halves, base, zones = chunks[t]
            if 1 in halves and len(injs) == 1:
                across = copy_after(across, token)
                injs.append(half_injections(1, [across, lax.ppermute(across, "line", by_core)]))
            lead, then = (2, 1) if t in z_first else (1, 2)
            splits = ((row[3], row[lead]), (row[then],), (row[0],))
            send, give, keep, *done = partial(
                near_flag,
                token,
                [injs[h] for h in halves],
                blocks,
                base,
                zones,
                splits,
                stages=stages,
            )
            sent[t] = lax.ppermute(send, "bus", swaps[t][0])
            kept[t] = (give, keep)
            token = keep
        else:
            ending[t - ended], stages[2] = stages[2], ()
            done = []
            for stage in ([stages[0], (), ()], [(), stages[1], ()]):
                if any(stage):
                    done += sums(near_flag, token, stage, high)
                    token = done[-1]
        done = iter(done)
        if stages[0]:
            moved[t - summed] = lax.ppermute(next(done), "bus", swaps[t - summed][1])
            own[t - summed] = next(done)
        if stages[1]:
            halves = chunks[t - shared][0]
            if len(halves) == 1:
                late[t - shared] = lax.ppermute(next(done), ("line", "bus"), to_side(halves[0]))
            else:
                late[t - shared] = lax.ppermute(next(done), "bus", swap_far)
            own[t - shared] = next(done)
        if stages[2]:
            flows[t - ended] = next(done)
    flows.update((t, add(*stage)) for t, stage in ending.items() if stage)
    first_flows = [
        jnp.concatenate([flows[t] for t in range(total) if chunks[t][0] == (half,)], axis=1)
        for half in range(2)
    ]
    flows = [flows[t] for t in range(total) if len(chunks[t][0]) == 2]
    return [jnp.where(near, *first_flows)] + flows


def solution(mesh):
    return jax.shard_map(
        body,
        mesh=mesh,
        in_specs=(
            P("line", "bus"),
            P(),
            P("line", "bus"),
            P("line", "bus"),
            P("line", "bus", None, None),
            P("line"),
        ),
        out_specs=(P("bus", "line"), P("line")),
        check_vma=False,
    )
```
